512 devices in a mesh: expert: 128 (over z, y, core), dp: 4 (over x).
Axes of the slice: x: 4, y: 8, z: 8, core: 2. Of those that a mesh axis runs over, the one named last changes fastest.
Arguments:
- grads: bfloat16 [4, 256, 128, 1536], P('dp', 'expert'), may hold values from -6 to 6
- master: float32 [128, 128, 1536], P('expert', 'dp'), may hold values from -0.12 to 0.12
- moment: float32 [128, 128, 1536], P('expert', 'dp'), may hold values from -0.4 to 0.4
- second: float32 [128, 128, 1536], P('expert', 'dp'), may hold values from 0.001 to 0.01
- old_place: int32 [128, 2], replicated, may hold values from 0 to 127, all different within a row
- new_place: int32 [128, 2], replicated, may hold values from 0 to 127, all different within a row
- owner_slot: int32 [128], replicated, may hold values from 0 to 127, as said below
Outputs:
- new_master: float32 [128, 128, 1536], P('expert', 'dp')
- new_moment: float32 [128, 128, 1536], P('expert', 'dp')
- new_second: float32 [128, 128, 1536], P('expert', 'dp')
- replicas: bfloat16 [256, 128, 1536], P('expert', 'dp')
The draws below stay inside these ranges and needn't reach their ends.
Inputs may be any that keep to these rules, and one draw needn't show every extreme that they name: `owner_slot`: distinct values; the expert's owner is device value // 1 of the expert axis, in its owner slot value % 1. Slots that no expert names hold unused state. `old_place`: each device's 2 slots name distinct experts; every expert is named by some slot. `new_place`: each device's 2 slots name distinct experts; every expert is named by some slot.
All inputs are finite; a program needn't handle non-finite values.
Results may differ from the reference program's by a relative error of at most 0.015.
Values may be sent and summed in bfloat16 or wider, within the bound.
No kernel may reach another device: no remote copies, remote signals or barrier semaphores. Data moves between devices by JAX's collectives and lax.ppermute only.
A program may use at most 64 MiB of HBM per device.

```python
import math
import jax
import jax.numpy as jnp
from jax import lax

H = 1536
ROWS = 128
EXPERTS = 128
OWN_MAX = 1
REP = 2
N_EXPERT = 128
N_DP = 4


def draw_owner_slot(key, part):
    key = jax.random.fold_in(key, 7)
    slot_total = N_EXPERT * OWN_MAX
    key_first, key_second = jax.random.split(key)
    middle_slots = jax.random.permutation(key_first, slot_total - 2)[:EXPERTS - 2] + 1
    chosen_slots = jnp.concatenate([jnp.array([0, slot_total - 1], jnp.int32), middle_slots.astype(jnp.int32)])
    return jax.random.permutation(key_second, chosen_slots).astype(jnp.int32)


def steps_of(rng, shape, cuts, smallest, high):
    gain, own = 1.0, jax.random.fold_in(rng, 6)
    for axis_at, shards_of in cuts:
        draws = jnp.exp(jax.random.uniform(jax.random.fold_in(own, axis_at), (shards_of,), jnp.float32, smallest / len(cuts), high / len(cuts)))
        gain = gain * jnp.repeat(draws, shape[axis_at] // shards_of).reshape([-1 if axis == axis_at else 1 for axis in range(len(shape))])
    return gain


def choose_distinct(rng, rows, amount, top, lift):
    order = jax.random.permutation(jax.random.fold_in(rng, 1), amount)
    pull = order
    for power in range(3):
        pull = pull * pull // amount
    pull = pull * lift // amount
    lots = jax.random.randint(jax.random.fold_in(rng, 2), (rows, amount), 0, 4096) + pull
    fixed_rows = jax.random.permutation(jax.random.fold_in(rng, 3), rows)[jnp.arange(amount) % rows]
    lots = jnp.where(jnp.arange(rows)[:, None] == fixed_rows[None, :], 1 << 14, lots)
    priority = lots * amount + jnp.arange(amount)
    return lax.top_k(priority.astype(jnp.int32), top)[1].astype(jnp.int32)


def bell_draw(key, shape, scale, most, pieces=(), dtype=jnp.bfloat16):
    entries = jax.random.normal(key, shape, jnp.float32) * scale
    if len(pieces) > 0:
        entries = steps_of(key, shape, pieces, -0.22, 0.18) * entries
    return jnp.clip(entries, min=-most, max=most).astype(dtype)


def setup_inputs(seed: int = 0) -> dict:
    splits = jax.random.split(jax.random.key(seed), 8)
    grads = bell_draw(splits[0], (N_DP, N_EXPERT * REP, ROWS, H), 1.0, 6.0, ((0, 4), (1, 128)))
    master = bell_draw(splits[1], (N_EXPERT * OWN_MAX, ROWS, H), 0.03, 0.12, ((0, 128), (1, 4)), jnp.float32)
    moment = bell_draw(splits[2], (N_EXPERT * OWN_MAX, ROWS, H), 0.1, 0.4, ((0, 128), (1, 4)), jnp.float32)
    second = jnp.clip(jnp.exp(math.log(0.01) - 2.30258502 * jax.random.uniform(splits[3], (N_EXPERT * OWN_MAX, ROWS, H), jnp.float32) ** steps_of(splits[3], (N_EXPERT * OWN_MAX, ROWS, H), ((0, 128), (1, 4)), -0.2, 0.2)), 0.001, 0.01)
    old_place = choose_distinct(splits[4], N_EXPERT, EXPERTS, REP, 256)
    new_place = choose_distinct(splits[5], N_EXPERT, EXPERTS, REP, 256)
    owner_slot = draw_owner_slot(jax.random.fold_in(splits[7], 71), 0)
    return {"grads": grads, "master": master, "moment": moment, "second": second, "old_place": old_place, "new_place": new_place, "owner_slot": owner_slot}


beta_first = 0.9
beta_second = 0.999
learn_rate = 0.02
weight_decay = 0.1
epsilon = 1e-08
scale_first = 1.0 - 0.9 ** 40
scale_second = 1.0 - 0.999 ** 40

def reference(grads, master, moment, second, old_place, new_place, owner_slot):
    flat_old = old_place.reshape(-1).astype(jnp.int32)
    expert_grad = jnp.zeros((EXPERTS, ROWS, H), jnp.float32)
    for member in range(N_DP):
        expert_grad = expert_grad + jax.ops.segment_sum(grads[member].astype(jnp.float32), flat_old, num_segments=EXPERTS)
    slot_grad = jnp.zeros(master.shape, jnp.float32).at[owner_slot.astype(jnp.int32)].set(expert_grad)
    new_moment = beta_first * moment + (1.0 - beta_first) * slot_grad
    new_second = beta_second * second + (1.0 - beta_second) * slot_grad * slot_grad
    update = new_moment / scale_first / (jnp.sqrt(new_second / scale_second) + epsilon)
    new_master = master - learn_rate * (update + weight_decay * master)
    chosen = owner_slot[new_place.reshape(-1).astype(jnp.int32)].astype(jnp.int32)
    replicas = new_master[chosen].astype(jnp.bfloat16)
    return (new_master, new_moment, new_second, replicas)
```

```python
import jax
import jax.numpy as jnp
from jax import lax
from jax.experimental import pallas as pl
from jax.experimental.pallas import tpu as pltpu
from jax.sharding import PartitionSpec as P

beta_first = 0.9
beta_second = 0.999
learn_rate = 0.02
weight_decay = 0.1
epsilon = 1e-08
scale_first = 1.0 - 0.9**40
scale_second = 1.0 - 0.999**40

LANES = 128


def adamw(master, moment, second, grad):
    new_moment = beta_first * moment + (1.0 - beta_first) * grad
    new_second = beta_second * second + (1.0 - beta_second) * grad * grad
    update = new_moment / scale_first / (jnp.sqrt(new_second / scale_second) + epsilon)
    new_master = master - learn_rate * (update + weight_decay * master)
    return new_master, new_moment, new_second


def pack_kernel(grads, master, moment, second, out):
    copies, slots, rows, cols = grads.shape
    quarters = out.shape[1] // rows
    tall = cols // quarters // LANES
    arrays = []
    for slot in range(slots):
        total = grads[0, slot].astype(jnp.float32)
        for copy in range(1, copies):
            total = total + grads[copy, slot].astype(jnp.float32)
        arrays.append(total)
    arrays += [master[0], moment[0], second[0]]
    for a, whole in enumerate(arrays):
        whole = whole.astype(jnp.bfloat16)
        for q in range(quarters):
            for i in range(tall):
                at = (q * tall + i) * LANES
                out[a * tall + i, q * rows : (q + 1) * rows, :] = whole[:, at : at + LANES]
    for i in range(len(arrays) * tall, out.shape[0]):
        out[i] = jnp.zeros(out.shape[1:], out.dtype)


def update_kernel(pieces, old_place, new_place, owner_slot, out):
    slots, devices = old_place.shape
    span = out.shape[2]
    tall = span // LANES
    experts = owner_slot.shape[1]

    def hot(rows, values):
        at = lax.broadcasted_iota(jnp.int32, (rows, values.shape[1]), 0)
        return (at == values).astype(jnp.bfloat16)

    def dot(a, b, dims):
        return lax.dot_general(a, b, (dims, ((), ())), preferred_element_type=jnp.float32)

    owners = hot(devices, owner_slot[...])
    grad = [jnp.zeros((devices, LANES), jnp.float32) for _ in range(tall)]
    for slot in range(slots):
        held = hot(experts, old_place[slot : slot + 1, :])
        route = dot(owners, held, ((1,), (0,))).astype(jnp.bfloat16)
        for i in range(tall):
            grad[i] = grad[i] + dot(route, pieces[slot * tall + i], ((1,), (0,)))
    fresh = []
    for i in range(tall):
        master, moment, second = (
            pieces[(slots + a) * tall + i].astype(jnp.float32) for a in range(3)
        )
        new_master, _, _ = adamw(master, moment, second, grad[i])
        fresh.append(new_master.astype(jnp.bfloat16))
        out[slots, :, i * LANES : (i + 1) * LANES] = grad[i].astype(jnp.bfloat16)
    for slot in range(slots):
        held = hot(experts, new_place[slot : slot + 1, :])
        route = dot(owners, held, ((1,), (0,))).astype(jnp.bfloat16)
        for i in range(tall):
            out[slot, :, i * LANES : (i + 1) * LANES] = dot(route, fresh[i], ((0,), (0,))).astype(
                jnp.bfloat16
            )
    for i in range(slots + 1, out.shape[0]):
        out[i] = jnp.zeros(out.shape[1:], out.dtype)


def finish_kernel(pieces, master, moment, second, new_master, new_moment, new_second, replicas):
    slots, rows, cols = replicas.shape
    span = pieces.shape[2]
    for q in range(cols // span):
        here, there = pl.ds(q * rows, rows), pl.ds(q * span, span)
        for slot in range(slots):
            replicas[slot, :, there] = pieces[slot, here, :]
        grad = pieces[slots, here, :].astype(jnp.float32)
        a, b, c = adamw(master[0, :, there], moment[0, :, there], second[0, :, there], grad)
        new_master[0, :, there] = a
        new_moment[0, :, there] = b
        new_second[0, :, there] = c


def on_device(grads, master, moment, second, old_place, new_place, owner_slot):
    devices = lax.axis_size("expert")
    copies = lax.axis_size("dp")
    _, slots, full_rows, cols = grads.shape
    rows = full_rows // copies
    span = rows * cols // devices
    tall = span // LANES
    in_vmem = pl.BlockSpec(memory_space=pltpu.VMEM)

    by_rows = grads.reshape(slots, copies, rows, cols).transpose(1, 0, 2, 3)
    mine = lax.all_to_all(by_rows, "dp", split_axis=0, concat_axis=0, tiled=True)
    lines = -(-(slots + 3) * tall // 16) * 16
    packed = pl.pallas_call(
        pack_kernel,
        out_shape=jax.ShapeDtypeStruct((lines, devices, LANES), jnp.bfloat16),
        in_specs=[in_vmem] * 4,
        out_specs=in_vmem,
        name="pack",
    )(mine, master, moment, second)
    pieces = lax.all_to_all(packed, "expert", split_axis=1, concat_axis=1, tiled=True)
    outbound = pl.pallas_call(
        update_kernel,
        out_shape=jax.ShapeDtypeStruct((slots + 2, devices, span), jnp.bfloat16),
        in_specs=[in_vmem] * 4,
        out_specs=in_vmem,
        name="update",
    )(pieces, old_place.T, new_place.T, owner_slot[None, :])
    received = lax.all_to_all(outbound, "expert", split_axis=1, concat_axis=1, tiled=True)
    return pl.pallas_call(
        finish_kernel,
        out_shape=[jax.ShapeDtypeStruct(master.shape, jnp.float32)] * 3
        + [jax.ShapeDtypeStruct((slots, rows, cols), jnp.bfloat16)],
        in_specs=[in_vmem] * 4,
        out_specs=[in_vmem] * 4,
        name="finish",
    )(received, master, moment, second)


def solution(mesh):
    placed = (
        P("dp", "expert", None, None),
        P("expert", "dp", None),
        P("expert", "dp", None),
        P("expert", "dp", None),
        P(),
        P(),
        P(),
    )
    return jax.shard_map(
        on_device,
        mesh=mesh,
        in_specs=placed,
        out_specs=(
            P("expert", "dp", None),
            P("expert", "dp", None),
            P("expert", "dp", None),
            P("expert", "dp", None),
        ),
        check_vma=False,
    )
```

```python
import jax
import jax.numpy as jnp
from jax import lax
from jax.experimental import pallas as pl
from jax.experimental.pallas import tpu as pltpu
from jax.sharding import PartitionSpec as P

beta_first = 0.9
beta_second = 0.999
learn_rate = 0.02
weight_decay = 0.1
epsilon = 1e-08
scale_first = 1.0 - 0.9**40
scale_second = 1.0 - 0.999**40

LANES = 128


def adamw(master, moment, second, grad):
    new_moment = beta_first * moment + (1.0 - beta_first) * grad
    new_second = beta_second * second + (1.0 - beta_second) * grad * grad
    update = new_moment / scale_first / (jnp.sqrt(new_second / scale_second) + epsilon)
    new_master = master - learn_rate * (update + weight_decay * master)
    return new_master, new_moment, new_second


def pack_kernel(grads, master, moment, second, out):
    copies, slots, rows, cols = grads.shape
    devices, lines, _ = out.shape
    quarters = devices // rows
    tall = cols // quarters // LANES
    for q in range(quarters):
        blocks = []
        spans = [pl.ds((q * tall + i) * LANES, LANES) for i in range(tall)]
        for slot in range(slots):
            for span in spans:
                total = grads[0, slot, :, span].astype(jnp.float32)
                for copy in range(1, copies):
                    total = total + grads[copy, slot, :, span].astype(jnp.float32)
                blocks.append(total)
        for state in (master, moment, second):
            blocks += [state[0, :, span] for span in spans]
        blocks += [jnp.zeros((rows, LANES), jnp.float32)] * (lines - len(blocks))
        stacked = jnp.transpose(jnp.stack(blocks, 0), (1, 0, 2))
        out[q * rows : (q + 1) * rows] = stacked.astype(out.dtype)


def hot(rows, values):
    at = lax.broadcasted_iota(jnp.int32, (rows, values.shape[1]), 0)
    return (at == values).astype(jnp.bfloat16)


def dot(a, b, dims):
    return lax.dot_general(a, b, (dims, ((), ())), preferred_element_type=jnp.float32)


def update_kernel(pieces, old_place, new_place, owner_slot, out, arrived, leaving):
    slots, devices = old_place.shape
    lines = pieces.shape[1]
    lines_out = leaving.shape[0] // devices
    tall = lines_out // (slots + 1)
    experts = owner_slot.shape[1]
    arrived[...] = pieces[...].reshape(arrived.shape).astype(jnp.float32)

    def line(at):
        return arrived[pl.ds(at, devices, stride=lines), :]

    def leave(at, value):
        leaving[pl.ds(at, devices, stride=lines_out), :] = value

    owners = hot(devices, owner_slot[...])
    grad = jnp.zeros((devices, tall * LANES), jnp.float32)
    for slot in range(slots):
        held = hot(experts, old_place[slot : slot + 1, :])
        route = dot(owners, held, ((1,), (0,))).astype(jnp.bfloat16)
        part = [line(slot * tall + i).astype(jnp.bfloat16) for i in range(tall)]
        grad = grad + dot(route, jnp.concatenate(part, 1), ((1,), (0,)))
    fresh = []
    for i in range(tall):
        mine = grad[:, i * LANES : (i + 1) * LANES]
        master, moment, second = (line((slots + a) * tall + i) for a in range(3))
        fresh.append(adamw(master, moment, second, mine)[0].astype(jnp.bfloat16))
        leave(slots * tall + i, mine)
    fresh = jnp.concatenate(fresh, 1)
    for slot in range(slots):
        held = hot(experts, new_place[slot : slot + 1, :])
        route = dot(owners, held, ((1,), (0,))).astype(jnp.bfloat16)
        chosen = dot(route, fresh, ((0,), (0,)))
        for i in range(tall):
            leave(slot * tall + i, chosen[:, i * LANES : (i + 1) * LANES])
    for at in range((slots + 1) * tall, lines_out):
        leave(at, jnp.zeros((devices, LANES), jnp.float32))
    out[...] = leaving[...].astype(out.dtype).reshape(out.shape)


def finish_kernel(pieces, master, moment, second, new_master, new_moment, new_second, replicas, arrived):
    slots, rows, cols = replicas.shape
    devices = pieces.shape[0]
    lines = arrived.shape[0] // devices
    quarters = devices // rows
    tall = cols // quarters // LANES
    arrived[...] = pieces[...].reshape(arrived.shape).astype(jnp.float32)
    for q in range(quarters):
        for i in range(tall):
            there = pl.ds((q * tall + i) * LANES, LANES)

            def line(array, q=q, i=i):
                return arrived[pl.ds(q * rows * lines + array * tall + i, rows, stride=lines), :]

            for slot in range(slots):
                replicas[slot, :, there] = line(slot).astype(replicas.dtype)
            new_master[0, :, there], new_moment[0, :, there], new_second[0, :, there] = adamw(
                master[0, :, there], moment[0, :, there], second[0, :, there], line(slots)
            )


def call(kernel, name, outs, args, scratch=()):
    in_vmem = pl.BlockSpec(memory_space=pltpu.VMEM)
    args = [pltpu.with_memory_space_constraint(arg, pltpu.VMEM) for arg in args]
    return pl.pallas_call(
        kernel,
        out_shape=outs,
        in_specs=[in_vmem] * len(args),
        out_specs=[in_vmem] * len(outs) if isinstance(outs, list) else in_vmem,
        scratch_shapes=scratch,
        name=name,
    )(*args)


def on_device(grads, master, moment, second, old_place, new_place, owner_slot):
    devices = lax.axis_size("expert")
    copies = lax.axis_size("dp")
    _, slots, full_rows, cols = grads.shape
    rows = full_rows // copies
    tall = rows * cols // devices // LANES
    lines = -(-(slots + 3) * tall // 16) * 16
    pairs = -(-(slots + 1) * tall // 2)
    state = (master, moment, second)

    by_rows = grads.reshape(slots, copies, rows, cols).transpose(1, 0, 2, 3)
    mine = lax.all_to_all(by_rows, "dp", split_axis=0, concat_axis=0, tiled=True)
    packed = call(
        pack_kernel, "pack", pltpu.VMEM((devices, lines, LANES), jnp.bfloat16), (mine, *state)
    )
    pieces = lax.all_to_all(packed, "expert", split_axis=0, concat_axis=0, tiled=True)
    outbound = call(
        update_kernel,
        "update",
        pltpu.VMEM((devices, pairs, 2, LANES), jnp.bfloat16),
        (pieces, old_place.T, new_place.T, owner_slot[None, :]),
        [
            pltpu.VMEM((devices * lines, LANES), jnp.float32),
            pltpu.VMEM((devices * pairs * 2, LANES), jnp.float32),
        ],
    )
    received = lax.all_to_all(outbound, "expert", split_axis=0, concat_axis=0, tiled=True)
    return call(
        finish_kernel,
        "finish",
        [jax.ShapeDtypeStruct(master.shape, jnp.float32)] * 3
        + [jax.ShapeDtypeStruct((slots, rows, cols), jnp.bfloat16)],
        (received, *state),
        [pltpu.VMEM((devices * pairs * 2, LANES), jnp.float32)],
    )


def solution(mesh):
    placed = (
        P("dp", "expert", None, None),
        P("expert", "dp", None),
        P("expert", "dp", None),
        P("expert", "dp", None),
        P(),
        P(),
        P(),
    )
    return jax.shard_map(
        on_device,
        mesh=mesh,
        in_specs=placed,
        out_specs=(
            P("expert", "dp", None),
            P("expert", "dp", None),
            P("expert", "dp", None),
            P("expert", "dp", None),
        ),
        check_vma=False,
    )
```

```python
import jax
import jax.numpy as jnp
from jax import lax
from jax.experimental import pallas as pl
from jax.experimental.pallas import tpu as pltpu
from jax.sharding import PartitionSpec as P

beta_first = 0.9
beta_second = 0.999
learn_rate = 0.02
weight_decay = 0.1
epsilon = 1e-08
scale_first = 1.0 - 0.9**40
scale_second = 1.0 - 0.999**40

LANES = 128


def adamw(master, moment, second, grad):
    new_moment = beta_first * moment + (1.0 - beta_first) * grad
    new_second = beta_second * second + (1.0 - beta_second) * grad * grad
    update = new_moment / scale_first / (jnp.sqrt(new_second / scale_second) + epsilon)
    new_master = master - learn_rate * (update + weight_decay * master)
    return new_master, new_moment, new_second


def hot(rows, values):
    at = lax.broadcasted_iota(jnp.int32, (rows, values.shape[1]), 0)
    return (at == values).astype(jnp.bfloat16)


def dot(a, b, dims):
    return lax.dot_general(a, b, (dims, ((), ())), preferred_element_type=jnp.float32)


def load_kernel(grads, places, by_rows, routes, held_places, sems):
    slots, copies = grads.shape[:2]
    index_copies = [
        pltpu.make_async_copy(place, held, sems.at[slots * copies + at])
        for at, (place, held) in enumerate(zip(places, held_places))
    ]
    grad_copies = [
        pltpu.make_async_copy(
            grads.at[slot, copy], by_rows.at[copy, slot], sems.at[slot * copies + copy]
        )
        for slot in range(slots)
        for copy in range(copies)
    ]
    for each in index_copies + grad_copies:
        each.start()
    for each in index_copies:
        each.wait()
    old_place, new_place, owner_slot = held_places
    _, owner_count, _ = routes.shape
    owners = hot(owner_count, owner_slot[...])
    for at, place in enumerate((old_place, new_place)):
        for slot in range(slots):
            held = hot(owner_slot.shape[1], place[slot : slot + 1, :])
            routes[at * slots + slot] = dot(owners, held, ((1,), (0,))).astype(routes.dtype)
    for each in grad_copies:
        each.wait()


def pack_kernel(grads, master, moment, second, out):
    copies, slots, rows, cols = grads.shape
    devices, lines, _ = out.shape
    quarters = devices // rows
    tall = cols // quarters // LANES
    for q in range(quarters):
        blocks = []
        spans = [pl.ds((q * tall + i) * LANES, LANES) for i in range(tall)]
        for slot in range(slots):
            for span in spans:
                total = grads[0, slot, :, span].astype(jnp.float32)
                for copy in range(1, copies):
                    total = total + grads[copy, slot, :, span].astype(jnp.float32)
                blocks.append(total)
        for state in (master, moment, second):
            blocks += [state[0, :, span] for span in spans]
        blocks += [jnp.zeros((rows, LANES), jnp.float32)] * (lines - len(blocks))
        stacked = jnp.transpose(jnp.stack(blocks, 0), (1, 0, 2))
        out[q * rows : (q + 1) * rows] = stacked.astype(out.dtype)


def update_kernel(pieces, routes, out, leaving):
    slots, devices = routes.shape[0] // 2, routes.shape[2]
    lines_out = leaving.shape[0] // devices
    tall = lines_out // (slots + 1)
    arrived = jnp.transpose(pieces[...], (1, 0, 2))

    def leave(at, value):
        leaving[pl.ds(at, devices, stride=lines_out), :] = value

    grad = jnp.zeros((devices, tall * LANES), jnp.float32)
    for slot in range(slots):
        part = [arrived[slot * tall + i] for i in range(tall)]
        grad = grad + dot(routes[slot], jnp.concatenate(part, 1), ((1,), (0,)))
    fresh = []
    for i in range(tall):
        mine = grad[:, i * LANES : (i + 1) * LANES]
        master, moment, second = (
            arrived[(slots + a) * tall + i].astype(jnp.float32) for a in range(3)
        )
        fresh.append(adamw(master, moment, second, mine)[0].astype(jnp.bfloat16))
        leave(slots * tall + i, mine)
    fresh = jnp.concatenate(fresh, 1)
    for slot in range(slots):
        chosen = dot(routes[slots + slot], fresh, ((0,), (0,)))
        for i in range(tall):
            leave(slot * tall + i, chosen[:, i * LANES : (i + 1) * LANES])
    for at in range((slots + 1) * tall, lines_out):
        leave(at, jnp.zeros((devices, LANES), jnp.float32))
    out[...] = leaving[...].astype(out.dtype).reshape(out.shape)


def finish_kernel(pieces, master, moment, second, new_master, new_moment, new_second, replicas, arrived):
    slots, rows, cols = replicas.shape
    devices = pieces.shape[0]
    lines = arrived.shape[0] // devices
    quarters = devices // rows
    tall = cols // quarters // LANES
    arrived[...] = pieces[...].reshape(arrived.shape).astype(jnp.float32)
    for q in range(quarters):
        for i in range(tall):
            there = pl.ds((q * tall + i) * LANES, LANES)

            def line(array, q=q, i=i):
                return arrived[pl.ds(q * rows * lines + array * tall + i, rows, stride=lines), :]

            for slot in range(slots):
                replicas[slot, :, there] = line(slot).astype(replicas.dtype)
            new_master[0, :, there], new_moment[0, :, there], new_second[0, :, there] = adamw(
                master[0, :, there], moment[0, :, there], second[0, :, there], line(slots)
            )


def call(kernel, name, outs, args, scratch=()):
    in_vmem = pl.BlockSpec(memory_space=pltpu.VMEM)
    args = [pltpu.with_memory_space_constraint(arg, pltpu.VMEM) for arg in args]
    return pl.pallas_call(
        kernel,
        out_shape=outs,
        in_specs=[in_vmem] * len(args),
        out_specs=[in_vmem] * len(outs) if isinstance(outs, list) else in_vmem,
        scratch_shapes=scratch,
        name=name,
    )(*args)


def load(grads, old_place, new_place, owner_slot):
    slots, copies, rows, cols = grads.shape
    devices = old_place.shape[0]
    places = (old_place.T, new_place.T, owner_slot[None, :])
    in_vmem = pl.BlockSpec(memory_space=pltpu.VMEM)
    anywhere = pl.BlockSpec(memory_space=pl.ANY)

    def kernel(grads, *refs):
        load_kernel(grads, refs[:3], refs[3], refs[4], refs[5:8], refs[8])

    return pl.pallas_call(
        kernel,
        out_shape=[
            pltpu.VMEM((copies, slots, rows, cols), grads.dtype),
            pltpu.VMEM((2 * slots, devices, devices), jnp.bfloat16),
        ],
        in_specs=[anywhere] * 4,
        out_specs=[in_vmem] * 2,
        scratch_shapes=[pltpu.VMEM(place.shape, place.dtype) for place in places]
        + [pltpu.SemaphoreType.DMA((slots * copies + 3,))],
        name="load",
    )(grads, *places)


def on_device(grads, master, moment, second, old_place, new_place, owner_slot):
    devices = lax.axis_size("expert")
    copies = lax.axis_size("dp")
    _, slots, full_rows, cols = grads.shape
    rows = full_rows // copies
    tall = rows * cols // devices // LANES
    lines = -(-(slots + 3) * tall // 16) * 16
    pairs = -(-(slots + 1) * tall // 2)
    state = (master, moment, second)

    by_rows, routes = load(grads.reshape(slots, copies, rows, cols), old_place, new_place, owner_slot)
    mine = lax.all_to_all(by_rows, "dp", split_axis=0, concat_axis=0, tiled=True)
    packed = call(
        pack_kernel, "pack", pltpu.VMEM((devices, lines, LANES), jnp.bfloat16), (mine, *state)
    )
    pieces = lax.all_to_all(packed, "expert", split_axis=0, concat_axis=0, tiled=True)
    outbound = call(
        update_kernel,
        "update",
        pltpu.VMEM((devices, pairs, 2, LANES), jnp.bfloat16),
        (pieces, routes),
        [pltpu.VMEM((devices * pairs * 2, LANES), jnp.float32)],
    )
    received = lax.all_to_all(outbound, "expert", split_axis=0, concat_axis=0, tiled=True)
    return call(
        finish_kernel,
        "finish",
        [jax.ShapeDtypeStruct(master.shape, jnp.float32)] * 3
        + [jax.ShapeDtypeStruct((slots, rows, cols), jnp.bfloat16)],
        (received, *state),
        [pltpu.VMEM((devices * pairs * 2, LANES), jnp.float32)],
    )


def solution(mesh):
    placed = (
        P("dp", "expert", None, None),
        P("expert", "dp", None),
        P("expert", "dp", None),
        P("expert", "dp", None),
        P(),
        P(),
        P(),
    )
    return jax.shard_map(
        on_device,
        mesh=mesh,
        in_specs=placed,
        out_specs=(
            P("expert", "dp", None),
            P("expert", "dp", None),
            P("expert", "dp", None),
            P("expert", "dp", None),
        ),
        check_vma=False,
    )
```

```python
import jax
import jax.numpy as jnp
from jax import lax
from jax.experimental import pallas as pl
from jax.experimental.pallas import tpu as pltpu
from jax.sharding import PartitionSpec as P

beta_first = 0.9
beta_second = 0.999
learn_rate = 0.02
weight_decay = 0.1
epsilon = 1e-08
scale_first = 1.0 - 0.9**40
scale_second = 1.0 - 0.999**40

LANES = 128


def adamw(master, moment, second, grad):
    new_moment = beta_first * moment + (1.0 - beta_first) * grad
    new_second = beta_second * second + (1.0 - beta_second) * grad * grad
    update = new_moment / scale_first / (jnp.sqrt(new_second / scale_second) + epsilon)
    new_master = master - learn_rate * (update + weight_decay * master)
    return new_master, new_moment, new_second


def hot(rows, values):
    at = lax.broadcasted_iota(jnp.int32, (rows, values.shape[1]), 0)
    return (at == values).astype(jnp.bfloat16)


def dot(a, b, dims):
    return lax.dot_general(a, b, (dims, ((), ())), preferred_element_type=jnp.float32)


def load_kernel(me, grads, places, by_rows, routes, held_places, sems):
    slots, copies = grads.shape[:2]
    index_copies = [
        pltpu.make_async_copy(place, held, sems.at[slots * copies + at])
        for at, (place, held) in enumerate(zip(places, held_places))
    ]
    grad_copies = [
        pltpu.make_async_copy(
            grads.at[slot, lax.rem(me + turn, copies)],
            by_rows[turn].at[slot],
            sems.at[slot * copies + turn],
        )
        for slot in range(slots)
        for turn in range(copies)
    ]
    for each in index_copies + grad_copies:
        each.start()
    for each in index_copies:
        each.wait()
    old_place, new_place, owner_slot = held_places
    _, owner_count, _ = routes.shape
    owners = hot(owner_count, owner_slot[...])
    for at, place in enumerate((old_place, new_place)):
        for slot in range(slots):
            held = hot(owner_slot.shape[1], place[slot : slot + 1, :])
            routes[at * slots + slot] = dot(owners, held, ((1,), (0,))).astype(routes.dtype)
    for each in grad_copies:
        each.wait()


def pack_kernel(*refs):
    *grads, master, moment, second, out = refs
    copies = len(grads)
    slots, rows, cols = grads[0].shape
    devices, lines, _ = out.shape
    quarters = devices // rows
    tall = cols // quarters // LANES
    for q in range(quarters):
        blocks = []
        spans = [pl.ds((q * tall + i) * LANES, LANES) for i in range(tall)]
        for slot in range(slots):
            for span in spans:
                total = grads[0][slot, :, span].astype(jnp.float32)
                for copy in range(1, copies):
                    total = total + grads[copy][slot, :, span].astype(jnp.float32)
                blocks.append(total)
        for state in (master, moment, second):
            blocks += [state[0, :, span] for span in spans]
        blocks += [jnp.zeros((rows, LANES), jnp.float32)] * (lines - len(blocks))
        stacked = jnp.transpose(jnp.stack(blocks, 0), (1, 0, 2))
        out[q * rows : (q + 1) * rows] = stacked.astype(out.dtype)


def update_kernel(pieces, routes, out, leaving):
    slots, devices = routes.shape[0] // 2, routes.shape[2]
    lines_out = leaving.shape[0] // devices
    tall = lines_out // (slots + 1)
    arrived = jnp.transpose(pieces[...], (1, 0, 2))

    def leave(at, value):
        leaving[pl.ds(at, devices, stride=lines_out), :] = value

    grad = jnp.zeros((devices, tall * LANES), jnp.float32)
    for slot in range(slots):
        part = [arrived[slot * tall + i] for i in range(tall)]
        grad = grad + dot(routes[slot], jnp.concatenate(part, 1), ((1,), (0,)))
    fresh = []
    for i in range(tall):
        mine = grad[:, i * LANES : (i + 1) * LANES]
        master, moment, second = (
            arrived[(slots + a) * tall + i].astype(jnp.float32) for a in range(3)
        )
        fresh.append(adamw(master, moment, second, mine)[0].astype(jnp.bfloat16))
        leave(slots * tall + i, mine)
    fresh = jnp.concatenate(fresh, 1)
    for slot in range(slots):
        chosen = dot(routes[slots + slot], fresh, ((0,), (0,)))
        for i in range(tall):
            leave(slot * tall + i, chosen[:, i * LANES : (i + 1) * LANES])
    for at in range((slots + 1) * tall, lines_out):
        leave(at, jnp.zeros((devices, LANES), jnp.float32))
    out[...] = leaving[...].astype(out.dtype).reshape(out.shape)


def finish_kernel(pieces, master, moment, second, new_master, new_moment, new_second, replicas, arrived):
    slots, rows, cols = replicas.shape
    devices = pieces.shape[0]
    lines = arrived.shape[0] // devices
    quarters = devices // rows
    tall = cols // quarters // LANES
    arrived[...] = pieces[...].reshape(arrived.shape).astype(jnp.float32)
    for q in range(quarters):
        for i in range(tall):
            there = pl.ds((q * tall + i) * LANES, LANES)

            def line(array, q=q, i=i):
                return arrived[pl.ds(q * rows * lines + array * tall + i, rows, stride=lines), :]

            for slot in range(slots):
                replicas[slot, :, there] = line(slot).astype(replicas.dtype)
            new_master[0, :, there], new_moment[0, :, there], new_second[0, :, there] = adamw(
                master[0, :, there], moment[0, :, there], second[0, :, there], line(slots)
            )


def call(kernel, name, outs, args, scratch=()):
    in_vmem = pl.BlockSpec(memory_space=pltpu.VMEM)
    args = [pltpu.with_memory_space_constraint(arg, pltpu.VMEM) for arg in args]
    return pl.pallas_call(
        kernel,
        out_shape=outs,
        in_specs=[in_vmem] * len(args),
        out_specs=[in_vmem] * len(outs) if isinstance(outs, list) else in_vmem,
        scratch_shapes=scratch,
        name=name,
    )(*args)


def load(grads, old_place, new_place, owner_slot):
    slots, copies, rows, cols = grads.shape
    devices = old_place.shape[0]
    places = (old_place.T, new_place.T, owner_slot[None, :])
    in_vmem = pl.BlockSpec(memory_space=pltpu.VMEM)
    anywhere = pl.BlockSpec(memory_space=pl.ANY)

    def kernel(grads, *refs):
        me = lax.axis_index("dp")
        load_kernel(me, grads, refs[:3], refs[3:7], refs[7], refs[8:11], refs[11])

    return pl.pallas_call(
        kernel,
        out_shape=[
            *[pltpu.VMEM((slots, rows, cols), grads.dtype)] * copies,
            pltpu.VMEM((2 * slots, devices, devices), jnp.bfloat16),
        ],
        in_specs=[anywhere] * 4,
        out_specs=[in_vmem] * (copies + 1),
        scratch_shapes=[pltpu.VMEM(place.shape, place.dtype) for place in places]
        + [pltpu.SemaphoreType.DMA((slots * copies + 3,))],
        name="load",
    )(grads, *places)


def on_device(grads, master, moment, second, old_place, new_place, owner_slot):
    devices = lax.axis_size("expert")
    copies = lax.axis_size("dp")
    _, slots, full_rows, cols = grads.shape
    rows = full_rows // copies
    tall = rows * cols // devices // LANES
    lines = -(-(slots + 3) * tall // 16) * 16
    pairs = -(-(slots + 1) * tall // 2)
    state = (master, moment, second)

    *by_rows, routes = load(grads.reshape(slots, copies, rows, cols), old_place, new_place, owner_slot)
    mine = [by_rows[0]]
    for turn in sorted(range(1, copies), key=lambda d: abs(copies - 2 * d)):
        moves = [(i, (i + turn) % copies) for i in range(copies)]
        mine.append(lax.ppermute(by_rows[turn], "dp", moves))
    packed = call(
        pack_kernel, "pack", pltpu.VMEM((devices, lines, LANES), jnp.bfloat16), (*mine, *state)
    )
    pieces = lax.all_to_all(packed, "expert", split_axis=0, concat_axis=0, tiled=True)
    outbound = call(
        update_kernel,
        "update",
        pltpu.VMEM((devices, pairs, 2, LANES), jnp.bfloat16),
        (pieces, routes),
        [pltpu.VMEM((devices * pairs * 2, LANES), jnp.float32)],
    )
    received = lax.all_to_all(outbound, "expert", split_axis=0, concat_axis=0, tiled=True)
    return call(
        finish_kernel,
        "finish",
        [jax.ShapeDtypeStruct(master.shape, jnp.float32)] * 3
        + [jax.ShapeDtypeStruct((slots, rows, cols), jnp.bfloat16)],
        (received, *state),
        [pltpu.VMEM((devices * pairs * 2, LANES), jnp.float32)],
    )


def solution(mesh):
    placed = (
        P("dp", "expert", None, None),
        P("expert", "dp", None),
        P("expert", "dp", None),
        P("expert", "dp", None),
        P(),
        P(),
        P(),
    )
    return jax.shard_map(
        on_device,
        mesh=mesh,
        in_specs=placed,
        out_specs=(
            P("expert", "dp", None),
            P("expert", "dp", None),
            P("expert", "dp", None),
            P("expert", "dp", None),
        ),
        check_vma=False,
    )
```

```python
import jax
import jax.numpy as jnp
from jax import lax
from jax.experimental import pallas as pl
from jax.experimental.pallas import tpu as pltpu
from jax.sharding import PartitionSpec as P

beta_first = 0.9
beta_second = 0.999
learn_rate = 0.02
weight_decay = 0.1
epsilon = 1e-08
scale_first = 1.0 - 0.9**40
scale_second = 1.0 - 0.999**40

LANES = 128


def adamw(master, moment, second, grad):
    new_moment = beta_first * moment + (1.0 - beta_first) * grad
    new_second = beta_second * second + (1.0 - beta_second) * grad * grad
    update = new_moment / scale_first / (jnp.sqrt(new_second / scale_second) + epsilon)
    new_master = master - learn_rate * (update + weight_decay * master)
    return new_master, new_moment, new_second


def hot(rows, values):
    at = lax.broadcasted_iota(jnp.int32, (rows, values.shape[1]), 0)
    return (at == values).astype(jnp.bfloat16)


def dot(a, b, dims):
    return lax.dot_general(a, b, (dims, ((), ())), preferred_element_type=jnp.float32)


def turns(copies, odd):
    return sorted(
        range(copies),
        key=lambda d: (d > 0, -min(d, copies - d), d if not odd else -d),
    )


def load_kernel(me, turned, grads, places, by_rows, routes, held_places, sems):
    slots, copies = grads.shape[:2]
    index_copies = [
        pltpu.make_async_copy(place, held, sems.at[slots * copies + at])
        for at, (place, held) in enumerate(zip(places, held_places))
    ]
    grad_copies = [
        pltpu.make_async_copy(
            grads.at[slot, lax.rem(me + turn, copies)],
            by_rows[n].at[slot],
            sems.at[slot * copies + n],
        )
        for slot in range(slots)
        for n, turn in enumerate(turned)
    ]
    for each in index_copies + grad_copies:
        each.start()
    for each in index_copies:
        each.wait()
    old_place, new_place, owner_slot = held_places
    _, owner_count, _ = routes.shape
    owners = hot(owner_count, owner_slot[...])
    for at, place in enumerate((old_place, new_place)):
        for slot in range(slots):
            held = hot(owner_slot.shape[1], place[slot : slot + 1, :])
            routes[at * slots + slot] = dot(owners, held, ((1,), (0,))).astype(routes.dtype)
    for each in grad_copies:
        each.wait()


def pack_kernel(*refs):
    *grads, master, moment, second, out = refs
    copies = len(grads)
    slots, rows, cols = grads[0].shape
    devices, lines, _ = out.shape
    quarters = devices // rows
    tall = cols // quarters // LANES
    for q in range(quarters):
        blocks = []
        spans = [pl.ds((q * tall + i) * LANES, LANES) for i in range(tall)]
        for slot in range(slots):
            for span in spans:
                total = grads[0][slot, :, span].astype(jnp.float32)
                for copy in range(1, copies):
                    total = total + grads[copy][slot, :, span].astype(jnp.float32)
                blocks.append(total)
        for state in (master, moment, second):
            blocks += [state[0, :, span] for span in spans]
        blocks += [jnp.zeros((rows, LANES), jnp.float32)] * (lines - len(blocks))
        stacked = jnp.transpose(jnp.stack(blocks, 0), (1, 0, 2))
        out[q * rows : (q + 1) * rows] = stacked.astype(out.dtype)


def update_kernel(pieces, routes, out, leaving):
    slots, devices = routes.shape[0] // 2, routes.shape[2]
    lines_out = leaving.shape[0] // devices
    tall = lines_out // (slots + 1)
    arrived = jnp.transpose(pieces[...], (1, 0, 2))

    def leave(at, value):
        leaving[pl.ds(at, devices, stride=lines_out), :] = value

    grad = jnp.zeros((devices, tall * LANES), jnp.float32)
    for slot in range(slots):
        part = [arrived[slot * tall + i] for i in range(tall)]
        grad = grad + dot(routes[slot], jnp.concatenate(part, 1), ((1,), (0,)))
    fresh = []
    for i in range(tall):
        mine = grad[:, i * LANES : (i + 1) * LANES]
        master, moment, second = (
            arrived[(slots + a) * tall + i].astype(jnp.float32) for a in range(3)
        )
        fresh.append(adamw(master, moment, second, mine)[0].astype(jnp.bfloat16))
        leave(slots * tall + i, mine)
    fresh = jnp.concatenate(fresh, 1)
    for slot in range(slots):
        chosen = dot(routes[slots + slot], fresh, ((0,), (0,)))
        for i in range(tall):
            leave(slot * tall + i, chosen[:, i * LANES : (i + 1) * LANES])
    for at in range((slots + 1) * tall, lines_out):
        leave(at, jnp.zeros((devices, LANES), jnp.float32))
    out[...] = leaving[...].astype(out.dtype).reshape(out.shape)


def finish_kernel(pieces, master, moment, second, new_master, new_moment, new_second, replicas, arrived):
    slots, rows, cols = replicas.shape
    devices = pieces.shape[0]
    lines = arrived.shape[0] // devices
    quarters = devices // rows
    tall = cols // quarters // LANES
    arrived[...] = pieces[...].reshape(arrived.shape).astype(jnp.float32)
    for q in range(quarters):
        for i in range(tall):
            there = pl.ds((q * tall + i) * LANES, LANES)

            def line(array, q=q, i=i):
                return arrived[pl.ds(q * rows * lines + array * tall + i, rows, stride=lines), :]

            for slot in range(slots):
                replicas[slot, :, there] = line(slot).astype(replicas.dtype)
            new_master[0, :, there], new_moment[0, :, there], new_second[0, :, there] = adamw(
                master[0, :, there], moment[0, :, there], second[0, :, there], line(slots)
            )


def call(kernel, name, outs, args, scratch=()):
    in_vmem = pl.BlockSpec(memory_space=pltpu.VMEM)
    args = [pltpu.with_memory_space_constraint(arg, pltpu.VMEM) for arg in args]
    return pl.pallas_call(
        kernel,
        out_shape=outs,
        in_specs=[in_vmem] * len(args),
        out_specs=[in_vmem] * len(outs) if isinstance(outs, list) else in_vmem,
        scratch_shapes=scratch,
        name=name,
    )(*args)


def load(grads, old_place, new_place, owner_slot):
    slots, copies, rows, cols = grads.shape
    devices = old_place.shape[0]
    places = (old_place.T, new_place.T, owner_slot[None, :])
    in_vmem = pl.BlockSpec(memory_space=pltpu.VMEM)
    anywhere = pl.BlockSpec(memory_space=pl.ANY)

    def kernel(grads, *refs):
        me = lax.axis_index("dp")
        odd = lax.rem(lax.axis_index("expert"), 2)
        turned = [a + odd * (b - a) for a, b in zip(turns(copies, 0), turns(copies, 1))]
        load_kernel(me, turned, grads, refs[:3], refs[3:7], refs[7], refs[8:11], refs[11])

    return pl.pallas_call(
        kernel,
        out_shape=[
            *[pltpu.VMEM((slots, rows, cols), grads.dtype)] * copies,
            pltpu.VMEM((2 * slots, devices, devices), jnp.bfloat16),
        ],
        in_specs=[anywhere] * 4,
        out_specs=[in_vmem] * (copies + 1),
        scratch_shapes=[pltpu.VMEM(place.shape, place.dtype) for place in places]
        + [pltpu.SemaphoreType.DMA((slots * copies + 3,))],
        name="load",
    )(grads, *places)


def on_device(grads, master, moment, second, old_place, new_place, owner_slot):
    devices = lax.axis_size("expert")
    copies = lax.axis_size("dp")
    _, slots, full_rows, cols = grads.shape
    rows = full_rows // copies
    tall = rows * cols // devices // LANES
    lines = -(-(slots + 3) * tall // 16) * 16
    pairs = -(-(slots + 1) * tall // 2)
    state = (master, moment, second)

    *by_rows, routes = load(grads.reshape(slots, copies, rows, cols), old_place, new_place, owner_slot)
    mine = [by_rows[0]]
    for n in range(1, copies):
        moves = [
            (k * copies + i, k * copies + (i + turns(copies, k % 2)[n]) % copies)
            for k in range(devices)
            for i in range(copies)
        ]
        mine.append(lax.ppermute(by_rows[n], ("expert", "dp"), moves))
    packed = call(
        pack_kernel, "pack", pltpu.VMEM((devices, lines, LANES), jnp.bfloat16), (*mine, *state)
    )
    pieces = lax.all_to_all(packed, "expert", split_axis=0, concat_axis=0, tiled=True)
    outbound = call(
        update_kernel,
        "update",
        pltpu.VMEM((devices, pairs, 2, LANES), jnp.bfloat16),
        (pieces, routes),
        [pltpu.VMEM((devices * pairs * 2, LANES), jnp.float32)],
    )
    received = lax.all_to_all(outbound, "expert", split_axis=0, concat_axis=0, tiled=True)
    return call(
        finish_kernel,
        "finish",
        [jax.ShapeDtypeStruct(master.shape, jnp.float32)] * 3
        + [jax.ShapeDtypeStruct((slots, rows, cols), jnp.bfloat16)],
        (received, *state),
        [pltpu.VMEM((devices * pairs * 2, LANES), jnp.float32)],
    )


def solution(mesh):
    placed = (
        P("dp", "expert", None, None),
        P("expert", "dp", None),
        P("expert", "dp", None),
        P("expert", "dp", None),
        P(),
        P(),
        P(),
    )
    return jax.shard_map(
        on_device,
        mesh=mesh,
        in_specs=placed,
        out_specs=(
            P("expert", "dp", None),
            P("expert", "dp", None),
            P("expert", "dp", None),
            P("expert", "dp", None),
        ),
        check_vma=False,
    )
```

```python
import functools

import jax
import jax.numpy as jnp
from jax import lax
from jax.experimental import pallas as pl
from jax.experimental.pallas import tpu as pltpu
from jax.sharding import PartitionSpec as P

beta_first = 0.9
beta_second = 0.999
learn_rate = 0.02
weight_decay = 0.1
epsilon = 1e-08
scale_first = 1.0 - 0.9**40
scale_second = 1.0 - 0.999**40

LANES = 128


def adamw(master, moment, second, grad):
    new_moment = beta_first * moment + (1.0 - beta_first) * grad
    new_second = beta_second * second + (1.0 - beta_second) * grad * grad
    update = new_moment / scale_first / (jnp.sqrt(new_second / scale_second) + epsilon)
    new_master = master - learn_rate * (update + weight_decay * master)
    return new_master, new_moment, new_second


def place_of(at):
    return ((7 - (at >> 4)) << 4) + (((4 - (at >> 1)) & 7) << 1) + (1 - (at & 1))


def hot(rows, values, label=lambda at: at):
    at = lax.broadcasted_iota(jnp.int32, (rows, values.shape[1]), 0)
    return (label(at) == values).astype(jnp.bfloat16)


def dot(a, b, dims):
    return lax.dot_general(a, b, (dims, ((), ())), preferred_element_type=jnp.float32)


def turns(copies, odd):
    return sorted(
        range(copies),
        key=lambda d: (d > 0, -min(d, copies - d), d if not odd else -d),
    )


def load_kernel(me, turned, grads, places, by_rows, routes, held_places, sems):
    slots, copies = grads.shape[:2]
    index_copies = [
        pltpu.make_async_copy(place, held, sems.at[slots * copies + at])
        for at, (place, held) in enumerate(zip(places, held_places))
    ]
    grad_copies = [
        pltpu.make_async_copy(
            grads.at[slot, lax.rem(me + turn, copies)],
            by_rows[n].at[slot],
            sems.at[slot * copies + n],
        )
        for slot in range(slots)
        for n, turn in enumerate(turned)
    ]
    for each in index_copies + grad_copies:
        each.start()
    for each in index_copies:
        each.wait()
    old_place, new_place, owner_slot = held_places
    _, owner_count, _ = routes.shape
    owners = hot(owner_count, owner_slot[...], place_of)
    natural = lax.broadcasted_iota(jnp.int32, (1, owner_count), 1)
    order = hot(owner_count, natural, place_of)
    for at, place in enumerate((old_place, new_place)):
        for slot in range(slots):
            held = hot(owner_slot.shape[1], place[slot : slot + 1, :])
            held = dot(held, order, ((1,), (1,))).astype(jnp.bfloat16)
            routes[at * slots + slot] = dot(owners, held, ((1,), (0,))).astype(routes.dtype)
    for each in grad_copies:
        each.wait()


def pack_kernel(*refs):
    *grads, master, moment, second, out = refs
    copies = len(grads)
    slots, rows, cols = grads[0].shape
    devices, lines, _ = out.shape
    quarters = devices // rows
    tall = cols // quarters // LANES
    for q in range(quarters):
        blocks = []
        spans = [pl.ds((q * tall + i) * LANES, LANES) for i in range(tall)]
        for slot in range(slots):
            for span in spans:
                total = grads[0][slot, :, span].astype(jnp.float32)
                for copy in range(1, copies):
                    total = total + grads[copy][slot, :, span].astype(jnp.float32)
                blocks.append(total)
        for state in (master, moment, second):
            blocks += [state[0, :, span] for span in spans]
        blocks += [jnp.zeros((rows, LANES), jnp.float32)] * (lines - len(blocks))
        stacked = jnp.transpose(jnp.stack(blocks, 0), (1, 0, 2))
        out[q * rows : (q + 1) * rows] = stacked.astype(out.dtype)


def update_kernel(pieces, routes, out, leaving):
    slots, devices = routes.shape[0] // 2, routes.shape[2]
    lines_out = out.shape[1] * out.shape[2]
    tall = lines_out // (slots + 1)
    arrived = jnp.transpose(pieces[...], (1, 0, 2))

    def leave(at, value):
        leaving[pl.ds(at, devices, stride=lines_out), :] = value

    grad = jnp.zeros((devices, tall * LANES), jnp.float32)
    for slot in range(slots):
        part = [arrived[slot * tall + i] for i in range(tall)]
        grad = grad + dot(routes[slot], jnp.concatenate(part, 1), ((1,), (0,)))
    fresh = []
    for i in range(tall):
        mine = grad[:, i * LANES : (i + 1) * LANES]
        master, moment, second = (
            arrived[(slots + a) * tall + i].astype(jnp.float32) for a in range(3)
        )
        fresh.append(adamw(master, moment, second, mine)[0].astype(jnp.bfloat16))
        leave(slots * tall + i, mine)
    fresh = jnp.concatenate(fresh, 1)
    for slot in range(slots):
        chosen = dot(routes[slots + slot], fresh, ((0,), (0,)))
        for i in range(tall):
            leave(slot * tall + i, chosen[:, i * LANES : (i + 1) * LANES])
    for at in range((slots + 1) * tall, lines_out):
        leave(at, jnp.zeros((devices, LANES), jnp.float32))
    out[...] = leaving[: devices * lines_out].astype(out.dtype).reshape(out.shape)


def finish_kernel(pieces, master, moment, second, new_master, new_moment, new_second, replicas, arrived):
    slots, rows, cols = replicas.shape
    devices = pieces.shape[0]
    lines = pieces.shape[1] * pieces.shape[2]
    quarters = devices // rows
    tall = cols // quarters // LANES
    arrived[: devices * lines] = pieces[...].reshape(devices * lines, LANES).astype(jnp.float32)
    for q in range(quarters):
        for i in range(tall):
            there = pl.ds((q * tall + i) * LANES, LANES)

            def line(array, q=q, i=i):
                return arrived[pl.ds(q * rows * lines + array * tall + i, rows, stride=lines), :]

            for slot in range(slots):
                replicas[slot, :, there] = line(slot).astype(replicas.dtype)
            new_master[0, :, there], new_moment[0, :, there], new_second[0, :, there] = adamw(
                master[0, :, there], moment[0, :, there], second[0, :, there], line(slots)
            )


def call(kernel, name, outs, args, scratch=()):
    in_vmem = pl.BlockSpec(memory_space=pltpu.VMEM)
    args = [pltpu.with_memory_space_constraint(arg, pltpu.VMEM) for arg in args]
    return pl.pallas_call(
        kernel,
        out_shape=outs,
        in_specs=[in_vmem] * len(args),
        out_specs=[in_vmem] * len(outs) if isinstance(outs, list) else in_vmem,
        scratch_shapes=scratch,
        name=name,
    )(*args)


def load(grads, old_place, new_place, owner_slot):
    slots, copies, rows, cols = grads.shape
    devices = old_place.shape[0]
    places = (old_place.T, new_place.T, owner_slot[None, :])
    in_vmem = pl.BlockSpec(memory_space=pltpu.VMEM)
    anywhere = pl.BlockSpec(memory_space=pl.ANY)

    def kernel(grads, *refs):
        me = lax.axis_index("dp")
        odd = lax.rem(lax.axis_index("expert"), 2)
        turned = [a + odd * (b - a) for a, b in zip(turns(copies, 0), turns(copies, 1))]
        load_kernel(me, turned, grads, refs[:3], refs[3:7], refs[7], refs[8:11], refs[11])

    return pl.pallas_call(
        kernel,
        out_shape=[
            *[pltpu.VMEM((slots, rows, cols), grads.dtype)] * copies,
            pltpu.VMEM((2 * slots, devices, devices), jnp.bfloat16),
        ],
        in_specs=[anywhere] * 4,
        out_specs=[in_vmem] * (copies + 1),
        scratch_shapes=[pltpu.VMEM(place.shape, place.dtype) for place in places]
        + [pltpu.SemaphoreType.DMA((slots * copies + 3,))],
        name="load",
    )(grads, *places)


def on_device(grads, master, moment, second, old_place, new_place, owner_slot):
    devices = lax.axis_size("expert")
    copies = lax.axis_size("dp")
    _, slots, full_rows, cols = grads.shape
    rows = full_rows // copies
    tall = rows * cols // devices // LANES
    lines = -(-(slots + 3) * tall // 16) * 16
    pairs = -(-(slots + 1) * tall // 2)
    state = (master, moment, second)
    message_lines = pltpu.VMEM(((devices + 8) * pairs * 2, LANES), jnp.float32)

    *by_rows, routes = load(grads.reshape(slots, copies, rows, cols), old_place, new_place, owner_slot)
    mine = [by_rows[0]]
    for n in range(1, copies):
        moves = [
            (k * copies + i, k * copies + (i + turns(copies, k % 2)[n]) % copies)
            for k in range(devices)
            for i in range(copies)
        ]
        mine.append(lax.ppermute(by_rows[n], ("expert", "dp"), moves))
    packed = call(
        pack_kernel, "pack", pltpu.VMEM((devices, lines, LANES), jnp.bfloat16), (*mine, *state)
    )
    exchange = functools.partial(
        lax.all_to_all,
        axis_name="expert",
        split_axis=0,
        concat_axis=0,
        tiled=True,
        axis_index_groups=[[place_of(at) for at in range(devices)]],
    )
    pieces = exchange(packed)
    outbound = call(
        update_kernel,
        "update",
        pltpu.VMEM((devices, pairs, 2, LANES), jnp.bfloat16),
        (pieces, routes),
        [message_lines],
    )
    received = exchange(outbound)
    return call(
        finish_kernel,
        "finish",
        [jax.ShapeDtypeStruct(master.shape, jnp.float32)] * 3
        + [jax.ShapeDtypeStruct((slots, rows, cols), jnp.bfloat16)],
        (received, *state),
        [message_lines],
    )


def solution(mesh):
    placed = (
        P("dp", "expert", None, None),
        P("expert", "dp", None),
        P("expert", "dp", None),
        P("expert", "dp", None),
        P(),
        P(),
        P(),
    )
    return jax.shard_map(
        on_device,
        mesh=mesh,
        in_specs=placed,
        out_specs=(
            P("expert", "dp", None),
            P("expert", "dp", None),
            P("expert", "dp", None),
            P("expert", "dp", None),
        ),
        check_vma=False,
    )
```

```python
import functools

import jax
import jax.numpy as jnp
from jax import lax
from jax.experimental import pallas as pl
from jax.experimental.pallas import tpu as pltpu
from jax.sharding import PartitionSpec as P

beta_first = 0.9
beta_second = 0.999
learn_rate = 0.02
weight_decay = 0.1
epsilon = 1e-08
scale_first = 1.0 - 0.9**40
scale_second = 1.0 - 0.999**40

LANES = 128


def adamw(master, moment, second, grad):
    new_moment = beta_first * moment + (1.0 - beta_first) * grad
    new_second = beta_second * second + (1.0 - beta_second) * grad * grad
    update = new_moment / scale_first / (jnp.sqrt(new_second / scale_second) + epsilon)
    new_master = master - learn_rate * (update + weight_decay * master)
    return new_master, new_moment, new_second


def place_of(at):
    return (((5 - (at >> 4)) & 7) << 4) + (((4 - (at >> 1)) & 7) << 1) + (1 - (at & 1))


def hot(rows, values, label=lambda at: at):
    at = lax.broadcasted_iota(jnp.int32, (rows, values.shape[1]), 0)
    return (label(at) == values).astype(jnp.bfloat16)


def dot(a, b, dims):
    return lax.dot_general(a, b, (dims, ((), ())), preferred_element_type=jnp.float32)


def turns(copies, odd):
    return sorted(
        range(copies),
        key=lambda d: (d > 0, -min(d, copies - d), d if not odd else -d),
    )


def load_kernel(me, turned, grads, places, by_rows, routes, held_places, sems):
    slots, copies = grads.shape[:2]
    index_copies = [
        pltpu.make_async_copy(place, held, sems.at[slots * copies + at])
        for at, (place, held) in enumerate(zip(places, held_places))
    ]
    grad_copies = [
        pltpu.make_async_copy(
            grads.at[slot, lax.rem(me + turn, copies)],
            by_rows[n].at[slot],
            sems.at[slot * copies + n],
        )
        for slot in range(slots)
        for n, turn in enumerate(turned)
    ]
    for each in index_copies + grad_copies:
        each.start()
    for each in index_copies:
        each.wait()
    old_place, new_place, owner_slot = held_places
    _, owner_count, _ = routes.shape
    owners = hot(owner_count, owner_slot[...], place_of)
    natural = lax.broadcasted_iota(jnp.int32, (1, owner_count), 1)
    order = hot(owner_count, natural, place_of)
    for at, place in enumerate((old_place, new_place)):
        for slot in range(slots):
            held = hot(owner_slot.shape[1], place[slot : slot + 1, :])
            held = dot(held, order, ((1,), (1,))).astype(jnp.bfloat16)
            routes[at * slots + slot] = dot(owners, held, ((1,), (0,))).astype(routes.dtype)
    for each in grad_copies:
        each.wait()


def pack_kernel(*refs):
    *grads, master, moment, second, out = refs
    copies = len(grads)
    slots, rows, cols = grads[0].shape
    devices, lines, _ = out.shape
    quarters = devices // rows
    tall = cols // quarters // LANES
    for q in range(quarters):
        blocks = []
        spans = [pl.ds((q * tall + i) * LANES, LANES) for i in range(tall)]
        for slot in range(slots):
            for span in spans:
                total = grads[0][slot, :, span].astype(jnp.float32)
                for copy in range(1, copies):
                    total = total + grads[copy][slot, :, span].astype(jnp.float32)
                blocks.append(total)
        for state in (master, moment, second):
            blocks += [state[0, :, span] for span in spans]
        blocks += [jnp.zeros((rows, LANES), jnp.float32)] * (lines - len(blocks))
        stacked = jnp.transpose(jnp.stack(blocks, 0), (1, 0, 2))
        out[q * rows : (q + 1) * rows] = stacked.astype(out.dtype)


def update_kernel(pieces, routes, out, leaving):
    slots, devices = routes.shape[0] // 2, routes.shape[2]
    lines_out = out.shape[1] * out.shape[2]
    tall = lines_out // (slots + 1)
    arrived = jnp.transpose(pieces[...], (1, 0, 2))

    def leave(at, value):
        leaving[pl.ds(at, devices, stride=lines_out), :] = value

    grad = jnp.zeros((devices, tall * LANES), jnp.float32)
    for slot in range(slots):
        part = [arrived[slot * tall + i] for i in range(tall)]
        grad = grad + dot(routes[slot], jnp.concatenate(part, 1), ((1,), (0,)))
    fresh = []
    for i in range(tall):
        mine = grad[:, i * LANES : (i + 1) * LANES]
        master, moment, second = (
            arrived[(slots + a) * tall + i].astype(jnp.float32) for a in range(3)
        )
        fresh.append(adamw(master, moment, second, mine)[0].astype(jnp.bfloat16))
        leave(slots * tall + i, mine)
    fresh = jnp.concatenate(fresh, 1)
    for slot in range(slots):
        chosen = dot(routes[slots + slot], fresh, ((0,), (0,)))
        for i in range(tall):
            leave(slot * tall + i, chosen[:, i * LANES : (i + 1) * LANES])
    for at in range((slots + 1) * tall, lines_out):
        leave(at, jnp.zeros((devices, LANES), jnp.float32))
    out[...] = leaving[: devices * lines_out].astype(out.dtype).reshape(out.shape)


def finish_kernel(pieces, master, moment, second, new_master, new_moment, new_second, replicas, arrived):
    slots, rows, cols = replicas.shape
    devices = pieces.shape[0]
    lines = pieces.shape[1] * pieces.shape[2]
    quarters = devices // rows
    tall = cols // quarters // LANES
    arrived[: devices * lines] = pieces[...].reshape(devices * lines, LANES).astype(jnp.float32)
    for q in range(quarters):
        for i in range(tall):
            there = pl.ds((q * tall + i) * LANES, LANES)

            def line(array, q=q, i=i):
                return arrived[pl.ds(q * rows * lines + array * tall + i, rows, stride=lines), :]

            for slot in range(slots):
                replicas[slot, :, there] = line(slot).astype(replicas.dtype)
            new_master[0, :, there], new_moment[0, :, there], new_second[0, :, there] = adamw(
                master[0, :, there], moment[0, :, there], second[0, :, there], line(slots)
            )


def call(kernel, name, outs, args, scratch=()):
    in_vmem = pl.BlockSpec(memory_space=pltpu.VMEM)
    args = [pltpu.with_memory_space_constraint(arg, pltpu.VMEM) for arg in args]
    return pl.pallas_call(
        kernel,
        out_shape=outs,
        in_specs=[in_vmem] * len(args),
        out_specs=[in_vmem] * len(outs) if isinstance(outs, list) else in_vmem,
        scratch_shapes=scratch,
        name=name,
    )(*args)


def load(grads, old_place, new_place, owner_slot):
    slots, copies, rows, cols = grads.shape
    devices = old_place.shape[0]
    places = (old_place.T, new_place.T, owner_slot[None, :])
    in_vmem = pl.BlockSpec(memory_space=pltpu.VMEM)
    anywhere = pl.BlockSpec(memory_space=pl.ANY)

    def kernel(grads, *refs):
        me = lax.axis_index("dp")
        odd = lax.rem(lax.axis_index("expert"), 2)
        turned = [a + odd * (b - a) for a, b in zip(turns(copies, 0), turns(copies, 1))]
        load_kernel(me, turned, grads, refs[:3], refs[3:7], refs[7], refs[8:11], refs[11])

    return pl.pallas_call(
        kernel,
        out_shape=[
            *[pltpu.VMEM((slots, rows, cols), grads.dtype)] * copies,
            pltpu.VMEM((2 * slots, devices, devices), jnp.bfloat16),
        ],
        in_specs=[anywhere] * 4,
        out_specs=[in_vmem] * (copies + 1),
        scratch_shapes=[pltpu.VMEM(place.shape, place.dtype) for place in places]
        + [pltpu.SemaphoreType.DMA((slots * copies + 3,))],
        name="load",
    )(grads, *places)


def on_device(grads, master, moment, second, old_place, new_place, owner_slot):
    devices = lax.axis_size("expert")
    copies = lax.axis_size("dp")
    _, slots, full_rows, cols = grads.shape
    rows = full_rows // copies
    tall = rows * cols // devices // LANES
    lines = -(-(slots + 3) * tall // 16) * 16
    pairs = -(-(slots + 1) * tall // 2)
    state = (master, moment, second)
    message_lines = pltpu.VMEM(((devices + 8) * pairs * 2, LANES), jnp.float32)

    *by_rows, routes = load(grads.reshape(slots, copies, rows, cols), old_place, new_place, owner_slot)
    mine = [by_rows[0]]
    for n in range(1, copies):
        moves = [
            (k * copies + i, k * copies + (i + turns(copies, k % 2)[n]) % copies)
            for k in range(devices)
            for i in range(copies)
        ]
        mine.append(lax.ppermute(by_rows[n], ("expert", "dp"), moves))
    packed = call(
        pack_kernel, "pack", pltpu.VMEM((devices, lines, LANES), jnp.bfloat16), (*mine, *state)
    )
    exchange = functools.partial(
        lax.all_to_all,
        axis_name="expert",
        split_axis=0,
        concat_axis=0,
        tiled=True,
        axis_index_groups=[[place_of(at) for at in range(devices)]],
    )
    pieces = exchange(packed)
    outbound = call(
        update_kernel,
        "update",
        pltpu.VMEM((devices, pairs, 2, LANES), jnp.bfloat16),
        (pieces, routes),
        [message_lines],
    )
    received = exchange(outbound)
    return call(
        finish_kernel,
        "finish",
        [jax.ShapeDtypeStruct(master.shape, jnp.float32)] * 3
        + [jax.ShapeDtypeStruct((slots, rows, cols), jnp.bfloat16)],
        (received, *state),
        [message_lines],
    )


def solution(mesh):
    placed = (
        P("dp", "expert", None, None),
        P("expert", "dp", None),
        P("expert", "dp", None),
        P("expert", "dp", None),
        P(),
        P(),
        P(),
    )
    return jax.shard_map(
        on_device,
        mesh=mesh,
        in_specs=placed,
        out_specs=(
            P("expert", "dp", None),
            P("expert", "dp", None),
            P("expert", "dp", None),
            P("expert", "dp", None),
        ),
        check_vma=False,
    )
```

```python
import functools

import jax
import jax.numpy as jnp
from jax import lax
from jax.experimental import pallas as pl
from jax.experimental.pallas import tpu as pltpu
from jax.sharding import PartitionSpec as P

beta_first = 0.9
beta_second = 0.999
learn_rate = 0.02
weight_decay = 0.1
epsilon = 1e-08
scale_first = 1.0 - 0.9**40
scale_second = 1.0 - 0.999**40

LANES = 128


def adamw(master, moment, second, grad):
    new_moment = beta_first * moment + (1.0 - beta_first) * grad
    new_second = beta_second * second + (1.0 - beta_second) * grad * grad
    update = new_moment / scale_first / (jnp.sqrt(new_second / scale_second) + epsilon)
    new_master = master - learn_rate * (update + weight_decay * master)
    return new_master, new_moment, new_second


def place_of(at):
    return (((5 - (at >> 4)) & 7) << 4) + (((4 - (at >> 1)) & 7) << 1) + (1 - (at & 1))


def hot(rows, values, label=lambda at: at):
    at = lax.broadcasted_iota(jnp.int32, (rows, values.shape[1]), 0)
    return (label(at) == values).astype(jnp.bfloat16)


def dot(a, b, dims):
    return lax.dot_general(a, b, (dims, ((), ())), preferred_element_type=jnp.float32)


def dp_place_of(at, copies):
    return (copies // 2 - at) % copies


def load_kernel(grads, places, by_rows, routes, held_places, sems):
    slots, copies = grads.shape[:2]
    index_copies = [
        pltpu.make_async_copy(place, held, sems.at[slots * copies + at])
        for at, (place, held) in enumerate(zip(places, held_places))
    ]
    grad_copies = [
        pltpu.make_async_copy(
            grads.at[slot, dp_place_of(at, copies)],
            by_rows.at[at, slot],
            sems.at[slot * copies + at],
        )
        for slot in range(slots)
        for at in range(copies)
    ]
    for each in index_copies + grad_copies:
        each.start()
    for each in index_copies:
        each.wait()
    old_place, new_place, owner_slot = held_places
    _, owner_count, _ = routes.shape
    owners = hot(owner_count, owner_slot[...], place_of)
    natural = lax.broadcasted_iota(jnp.int32, (1, owner_count), 1)
    order = hot(owner_count, natural, place_of)
    for at, place in enumerate((old_place, new_place)):
        for slot in range(slots):
            held = hot(owner_slot.shape[1], place[slot : slot + 1, :])
            held = dot(held, order, ((1,), (1,))).astype(jnp.bfloat16)
            routes[at * slots + slot] = dot(owners, held, ((1,), (0,))).astype(routes.dtype)
    for each in grad_copies:
        each.wait()


def pack_kernel(grads, master, moment, second, out):
    copies, slots, rows, cols = grads.shape
    devices, lines, _ = out.shape
    quarters = devices // rows
    tall = cols // quarters // LANES
    for q in range(quarters):
        blocks = []
        spans = [pl.ds((q * tall + i) * LANES, LANES) for i in range(tall)]
        for slot in range(slots):
            for span in spans:
                total = grads[0, slot, :, span].astype(jnp.float32)
                for copy in range(1, copies):
                    total = total + grads[copy, slot, :, span].astype(jnp.float32)
                blocks.append(total)
        for state in (master, moment, second):
            blocks += [state[0, :, span] for span in spans]
        blocks += [jnp.zeros((rows, LANES), jnp.float32)] * (lines - len(blocks))
        stacked = jnp.transpose(jnp.stack(blocks, 0), (1, 0, 2))
        out[q * rows : (q + 1) * rows] = stacked.astype(out.dtype)


def update_kernel(pieces, routes, out, leaving):
    slots, devices = routes.shape[0] // 2, routes.shape[2]
    lines_out = out.shape[1] * out.shape[2]
    tall = lines_out // (slots + 1)
    arrived = jnp.transpose(pieces[...], (1, 0, 2))

    def leave(at, value):
        leaving[pl.ds(at, devices, stride=lines_out), :] = value

    grad = jnp.zeros((devices, tall * LANES), jnp.float32)
    for slot in range(slots):
        part = [arrived[slot * tall + i] for i in range(tall)]
        grad = grad + dot(routes[slot], jnp.concatenate(part, 1), ((1,), (0,)))
    fresh = []
    for i in range(tall):
        mine = grad[:, i * LANES : (i + 1) * LANES]
        master, moment, second = (
            arrived[(slots + a) * tall + i].astype(jnp.float32) for a in range(3)
        )
        fresh.append(adamw(master, moment, second, mine)[0].astype(jnp.bfloat16))
        leave(slots * tall + i, mine)
    fresh = jnp.concatenate(fresh, 1)
    for slot in range(slots):
        chosen = dot(routes[slots + slot], fresh, ((0,), (0,)))
        for i in range(tall):
            leave(slot * tall + i, chosen[:, i * LANES : (i + 1) * LANES])
    for at in range((slots + 1) * tall, lines_out):
        leave(at, jnp.zeros((devices, LANES), jnp.float32))
    out[...] = leaving[: devices * lines_out].astype(out.dtype).reshape(out.shape)


def finish_kernel(pieces, master, moment, second, new_master, new_moment, new_second, replicas, arrived):
    slots, rows, cols = replicas.shape
    devices = pieces.shape[0]
    lines = pieces.shape[1] * pieces.shape[2]
    quarters = devices // rows
    tall = cols // quarters // LANES
    arrived[: devices * lines] = pieces[...].reshape(devices * lines, LANES).astype(jnp.float32)
    for q in range(quarters):
        for i in range(tall):
            there = pl.ds((q * tall + i) * LANES, LANES)

            def line(array, q=q, i=i):
                return arrived[pl.ds(q * rows * lines + array * tall + i, rows, stride=lines), :]

            for slot in range(slots):
                replicas[slot, :, there] = line(slot).astype(replicas.dtype)
            new_master[0, :, there], new_moment[0, :, there], new_second[0, :, there] = adamw(
                master[0, :, there], moment[0, :, there], second[0, :, there], line(slots)
            )


def call(kernel, name, outs, args, scratch=()):
    in_vmem = pl.BlockSpec(memory_space=pltpu.VMEM)
    args = [pltpu.with_memory_space_constraint(arg, pltpu.VMEM) for arg in args]
    return pl.pallas_call(
        kernel,
        out_shape=outs,
        in_specs=[in_vmem] * len(args),
        out_specs=[in_vmem] * len(outs) if isinstance(outs, list) else in_vmem,
        scratch_shapes=scratch,
        name=name,
    )(*args)


def load(grads, old_place, new_place, owner_slot):
    slots, copies, rows, cols = grads.shape
    devices = old_place.shape[0]
    places = (old_place.T, new_place.T, owner_slot[None, :])
    in_vmem = pl.BlockSpec(memory_space=pltpu.VMEM)
    anywhere = pl.BlockSpec(memory_space=pl.ANY)

    def kernel(grads, *refs):
        load_kernel(grads, refs[:3], refs[3], refs[4], refs[5:8], refs[8])

    return pl.pallas_call(
        kernel,
        out_shape=[
            pltpu.VMEM((copies, slots, rows, cols), grads.dtype),
            pltpu.VMEM((2 * slots, devices, devices), jnp.bfloat16),
        ],
        in_specs=[anywhere] * 4,
        out_specs=[in_vmem] * 2,
        scratch_shapes=[pltpu.VMEM(place.shape, place.dtype) for place in places]
        + [pltpu.SemaphoreType.DMA((slots * copies + 3,))],
        name="load",
    )(grads, *places)


def on_device(grads, master, moment, second, old_place, new_place, owner_slot):
    devices = lax.axis_size("expert")
    copies = lax.axis_size("dp")
    _, slots, full_rows, cols = grads.shape
    rows = full_rows // copies
    tall = rows * cols // devices // LANES
    lines = -(-(slots + 3) * tall // 16) * 16
    pairs = -(-(slots + 1) * tall // 2)
    state = (master, moment, second)
    message_lines = pltpu.VMEM(((devices + 8) * pairs * 2, LANES), jnp.float32)

    by_rows, routes = load(grads.reshape(slots, copies, rows, cols), old_place, new_place, owner_slot)
    mine = lax.all_to_all(
        by_rows,
        "dp",
        split_axis=0,
        concat_axis=0,
        tiled=True,
        axis_index_groups=[[dp_place_of(at, copies) for at in range(copies)]],
    )
    packed = call(
        pack_kernel, "pack", pltpu.VMEM((devices, lines, LANES), jnp.bfloat16), (mine, *state)
    )
    exchange = functools.partial(
        lax.all_to_all,
        axis_name="expert",
        split_axis=0,
        concat_axis=0,
        tiled=True,
        axis_index_groups=[[place_of(at) for at in range(devices)]],
    )
    pieces = exchange(packed)
    outbound = call(
        update_kernel,
        "update",
        pltpu.VMEM((devices, pairs, 2, LANES), jnp.bfloat16),
        (pieces, routes),
        [message_lines],
    )
    received = exchange(outbound)
    return call(
        finish_kernel,
        "finish",
        [jax.ShapeDtypeStruct(master.shape, jnp.float32)] * 3
        + [jax.ShapeDtypeStruct((slots, rows, cols), jnp.bfloat16)],
        (received, *state),
        [message_lines],
    )


def solution(mesh):
    placed = (
        P("dp", "expert", None, None),
        P("expert", "dp", None),
        P("expert", "dp", None),
        P("expert", "dp", None),
        P(),
        P(),
        P(),
    )
    return jax.shard_map(
        on_device,
        mesh=mesh,
        in_specs=placed,
        out_specs=(
            P("expert", "dp", None),
            P("expert", "dp", None),
            P("expert", "dp", None),
            P("expert", "dp", None),
        ),
        check_vma=False,
    )
```

```python
import functools

import jax
import jax.numpy as jnp
from jax import lax
from jax.experimental import pallas as pl
from jax.experimental.pallas import tpu as pltpu
from jax.sharding import PartitionSpec as P

beta_first = 0.9
beta_second = 0.999
learn_rate = 0.02
weight_decay = 0.1
epsilon = 1e-08
scale_first = 1.0 - 0.9**40
scale_second = 1.0 - 0.999**40

LANES = 128


def adamw(master, moment, second, grad):
    new_moment = beta_first * moment + (1.0 - beta_first) * grad
    new_second = beta_second * second + (1.0 - beta_second) * grad * grad
    root = jnp.sqrt(new_second * (1.0 / scale_second))
    update = new_moment * (1.0 / scale_first) / (root + epsilon)
    new_master = master - learn_rate * (update + weight_decay * master)
    return new_master, new_moment, new_second


def place_of(at):
    return (((5 - (at >> 4)) & 7) << 4) + (((4 - (at >> 1)) & 7) << 1) + (1 - (at & 1))


def hot(rows, values, label=lambda at: at):
    at = lax.broadcasted_iota(jnp.int32, (rows, values.shape[1]), 0)
    return (label(at) == values).astype(jnp.bfloat16)


def dot(a, b, dims):
    return lax.dot_general(a, b, (dims, ((), ())), preferred_element_type=jnp.float32)


def dp_place_of(at, copies):
    return (copies // 2 - at) % copies


def load_kernel(grads, places, by_rows, routes, held_places, sems):
    slots, copies = grads.shape[:2]
    index_copies = [
        pltpu.make_async_copy(place, held, sems.at[slots * copies + at])
        for at, (place, held) in enumerate(zip(places, held_places))
    ]
    grad_copies = [
        pltpu.make_async_copy(
            grads.at[slot, dp_place_of(at, copies)],
            by_rows.at[at, slot],
            sems.at[slot * copies + at],
        )
        for slot in range(slots)
        for at in range(copies)
    ]
    for each in index_copies + grad_copies:
        each.start()
    for each in index_copies:
        each.wait()
    old_place, new_place, owner_slot = held_places
    _, owner_count, _ = routes.shape
    owners = hot(owner_count, owner_slot[...], place_of)
    natural = lax.broadcasted_iota(jnp.int32, (1, owner_count), 1)
    order = hot(owner_count, natural, place_of)
    for at, place in enumerate((old_place, new_place)):
        for slot in range(slots):
            held = hot(owner_slot.shape[1], place[slot : slot + 1, :])
            held = dot(held, order, ((1,), (1,))).astype(jnp.bfloat16)
            routes[at * slots + slot] = dot(owners, held, ((1,), (0,))).astype(routes.dtype)
    for each in grad_copies:
        each.wait()


def pack_kernel(grads, master, moment, second, out):
    copies, slots, rows, cols = grads.shape
    devices, lines, _ = out.shape
    quarters = devices // rows
    tall = cols // quarters // LANES
    for q in range(quarters):
        blocks = []
        spans = [pl.ds((q * tall + i) * LANES, LANES) for i in range(tall)]
        for slot in range(slots):
            for span in spans:
                total = grads[0, slot, :, span].astype(jnp.float32)
                for copy in range(1, copies):
                    total = total + grads[copy, slot, :, span].astype(jnp.float32)
                blocks.append(total)
        for state in (master, moment, second):
            blocks += [state[0, :, span] for span in spans]
        blocks += [jnp.zeros((rows, LANES), jnp.float32)] * (lines - len(blocks))
        stacked = jnp.transpose(jnp.stack(blocks, 0), (1, 0, 2))
        out[q * rows : (q + 1) * rows] = stacked.astype(out.dtype)


def update_kernel(pieces, routes, out, leaving):
    slots, devices = routes.shape[0] // 2, routes.shape[2]
    lines_out = out.shape[1] * out.shape[2]
    tall = lines_out // (slots + 1)
    arrived = jnp.transpose(pieces[...], (1, 0, 2))

    def leave(at, value):
        leaving[pl.ds(at, devices, stride=lines_out), :] = value

    grad = jnp.zeros((devices, tall * LANES), jnp.float32)
    for slot in range(slots):
        part = [arrived[slot * tall + i] for i in range(tall)]
        grad = grad + dot(routes[slot], jnp.concatenate(part, 1), ((1,), (0,)))
    fresh = []
    for i in range(tall):
        mine = grad[:, i * LANES : (i + 1) * LANES]
        master, moment, second = (
            arrived[(slots + a) * tall + i].astype(jnp.float32) for a in range(3)
        )
        fresh.append(adamw(master, moment, second, mine)[0].astype(jnp.bfloat16))
        leave(slots * tall + i, mine)
    fresh = jnp.concatenate(fresh, 1)
    for slot in range(slots):
        chosen = dot(routes[slots + slot], fresh, ((0,), (0,)))
        for i in range(tall):
            leave(slot * tall + i, chosen[:, i * LANES : (i + 1) * LANES])
    for at in range((slots + 1) * tall, lines_out):
        leave(at, jnp.zeros((devices, LANES), jnp.float32))
    out[...] = leaving[: devices * lines_out].astype(out.dtype).reshape(out.shape)


def finish_kernel(pieces, master, moment, second, new_master, new_moment, new_second, replicas, arrived):
    slots, rows, cols = replicas.shape
    devices = pieces.shape[0]
    lines = pieces.shape[1] * pieces.shape[2]
    quarters = devices // rows
    tall = cols // quarters // LANES
    arrived[: devices * lines] = pieces[...].reshape(devices * lines, LANES).astype(jnp.float32)
    for q in range(quarters):
        for i in range(tall):
            there = pl.ds((q * tall + i) * LANES, LANES)

            def line(array, q=q, i=i):
                return arrived[pl.ds(q * rows * lines + array * tall + i, rows, stride=lines), :]

            for slot in range(slots):
                replicas[slot, :, there] = line(slot).astype(replicas.dtype)
            new_master[0, :, there], new_moment[0, :, there], new_second[0, :, there] = adamw(
                master[0, :, there], moment[0, :, there], second[0, :, there], line(slots)
            )


def call(kernel, name, outs, args, scratch=()):
    in_vmem = pl.BlockSpec(memory_space=pltpu.VMEM)
    args = [pltpu.with_memory_space_constraint(arg, pltpu.VMEM) for arg in args]
    return pl.pallas_call(
        kernel,
        out_shape=outs,
        in_specs=[in_vmem] * len(args),
        out_specs=[in_vmem] * len(outs) if isinstance(outs, list) else in_vmem,
        scratch_shapes=scratch,
        name=name,
    )(*args)


def load(grads, old_place, new_place, owner_slot):
    slots, copies, rows, cols = grads.shape
    devices = old_place.shape[0]
    places = (old_place.T, new_place.T, owner_slot[None, :])
    in_vmem = pl.BlockSpec(memory_space=pltpu.VMEM)
    anywhere = pl.BlockSpec(memory_space=pl.ANY)

    def kernel(grads, *refs):
        load_kernel(grads, refs[:3], refs[3], refs[4], refs[5:8], refs[8])

    return pl.pallas_call(
        kernel,
        out_shape=[
            pltpu.VMEM((copies, slots, rows, cols), grads.dtype),
            pltpu.VMEM((2 * slots, devices, devices), jnp.bfloat16),
        ],
        in_specs=[anywhere] * 4,
        out_specs=[in_vmem] * 2,
        scratch_shapes=[pltpu.VMEM(place.shape, place.dtype) for place in places]
        + [pltpu.SemaphoreType.DMA((slots * copies + 3,))],
        name="load",
    )(grads, *places)


def on_device(grads, master, moment, second, old_place, new_place, owner_slot):
    devices = lax.axis_size("expert")
    copies = lax.axis_size("dp")
    _, slots, full_rows, cols = grads.shape
    rows = full_rows // copies
    tall = rows * cols // devices // LANES
    lines = -(-(slots + 3) * tall // 16) * 16
    pairs = -(-(slots + 1) * tall // 2)
    state = (master, moment, second)
    message_lines = pltpu.VMEM(((devices + 8) * pairs * 2, LANES), jnp.float32)

    by_rows, routes = load(grads.reshape(slots, copies, rows, cols), old_place, new_place, owner_slot)
    mine = lax.all_to_all(
        by_rows,
        "dp",
        split_axis=0,
        concat_axis=0,
        tiled=True,
        axis_index_groups=[[dp_place_of(at, copies) for at in range(copies)]],
    )
    packed = call(
        pack_kernel, "pack", pltpu.VMEM((devices, lines, LANES), jnp.bfloat16), (mine, *state)
    )
    exchange = functools.partial(
        lax.all_to_all,
        axis_name="expert",
        split_axis=0,
        concat_axis=0,
        tiled=True,
        axis_index_groups=[[place_of(at) for at in range(devices)]],
    )
    pieces = exchange(packed)
    outbound = call(
        update_kernel,
        "update",
        pltpu.VMEM((devices, pairs, 2, LANES), jnp.bfloat16),
        (pieces, routes),
        [message_lines],
    )
    received = exchange(outbound)
    return call(
        finish_kernel,
        "finish",
        [jax.ShapeDtypeStruct(master.shape, jnp.float32)] * 3
        + [jax.ShapeDtypeStruct((slots, rows, cols), jnp.bfloat16)],
        (received, *state),
        [message_lines],
    )


def solution(mesh):
    placed = (
        P("dp", "expert", None, None),
        P("expert", "dp", None),
        P("expert", "dp", None),
        P("expert", "dp", None),
        P(),
        P(),
        P(),
    )
    return jax.shard_map(
        on_device,
        mesh=mesh,
        in_specs=placed,
        out_specs=(
            P("expert", "dp", None),
            P("expert", "dp", None),
            P("expert", "dp", None),
            P("expert", "dp", None),
        ),
        check_vma=False,
    )
```
